512 devices in a mesh: sec: 2 (over x_lo), row: 16 (over y, x_hi), voc: 16 (over z, core).
Axes of the slice: x: 4 (x_hi: 2, x_lo: 2; x = x_hi * 2 + x_lo), y: 8, z: 8, core: 2. Of those that a mesh axis runs over, the one named last changes fastest.
Arguments:
- hidden: bfloat16 [448, 4096], P(('sec', 'row')), may hold values from -60 to 60
- head_weight: bfloat16 [4096, 131072], P(None, ('row', 'voc')), may hold values from -6 to 6
- teacher_logits: bfloat16 [448, 131072], P(None, ('row', 'voc', 'sec')), may hold values from -60 to 300
- lengths: int32 [32], P(('sec', 'row')), may hold values from 1 to 14
Outputs:
- grad_hidden: bfloat16 [448, 4096], P(('sec', 'row'), 'voc')
- loss_value: float32 [], replicated
The draws below stay inside these ranges and needn't reach their ends.
All inputs are finite; a program needn't handle non-finite values.
Results may differ from the reference program's by a relative error of at most 0.0049.
Values may be sent and summed in bfloat16 or wider, within the bound.
No kernel may reach another device: no remote copies, remote signals or barrier semaphores. Data moves between devices by JAX's collectives and lax.ppermute only.
A program may use at most 64 MiB of HBM per device.

```python
import jax
import jax.numpy as jnp
from jax import lax

D = 4096
TOK_DEV = 14
V = 131072
GROUPS = 32
TOKENS = 448


def draw_hidden(key, part):
    key = jax.random.fold_in(key, 11)
    second_key = jax.random.fold_in(key, 1)
    values = jnp.clip(3.0 * jax.random.normal(second_key, (TOKENS, D), jnp.float32), -15.0, 15.0)
    return values.astype(jnp.bfloat16)


def draw_head_weight(key, part):
    key = jax.random.fold_in(key, 12)
    second_key = jax.random.fold_in(key, 1)
    spread = D ** (-0.5)
    values = jnp.clip(spread * jax.random.normal(second_key, (D, V), jnp.float32), -6.0 * spread, 6.0 * spread)
    return values.astype(jnp.bfloat16)


def draw_teacher_logits(key, part):
    key = jax.random.fold_in(key, 13)
    second_key = jax.random.fold_in(key, 1)
    values = jnp.clip(3.0 * jax.random.normal(second_key, (TOKENS, V), jnp.float32), -18.0, 18.0)
    return values.astype(jnp.bfloat16)


def set_ends(array, own_key, smallest, largest):
    extent = array.shape
    spot = [jax.random.randint(jax.random.fold_in(own_key, axis), (), 0, extent[axis]) for axis in range(len(extent))]
    array = array.at[tuple(spot)].set(smallest)
    longest = extent.index(max(extent))
    spot[longest] = (spot[longest] + 1) % extent[longest]
    return array.at[tuple(spot)].set(largest)


def setup_inputs(seed: int = 0) -> dict:
    arg_keys = jax.random.split(jax.random.key(seed), 5)
    return {
        "hidden": draw_hidden(jax.random.fold_in(arg_keys[4], 71), 0),
        "head_weight": draw_head_weight(jax.random.fold_in(arg_keys[4], 71), 0),
        "teacher_logits": draw_teacher_logits(jax.random.fold_in(arg_keys[4], 71), 0),
        "lengths": set_ends(jax.random.randint(arg_keys[3], (GROUPS,), 1, TOK_DEV + 1), jax.random.fold_in(arg_keys[3], 1), 1, TOK_DEV).astype(jnp.int32),
    }


loss_scale = 131072.0


def log_normalize(values):
    row_top = jnp.max(values, axis=1, keepdims=True)
    row_total = jnp.sum(jnp.exp(values - row_top), axis=1, keepdims=True)
    return values - (row_top + jnp.log(row_total))


def reference(hidden, head_weight, teacher_logits, lengths):
    positions = jnp.arange(TOK_DEV, dtype=jnp.int32)
    token_valid = (positions[None, :] < lengths[:, None]).reshape(TOKENS).astype(jnp.float32)[:, None]
    student_logits = jnp.dot(hidden, head_weight, preferred_element_type=jnp.float32)
    log_student = log_normalize(student_logits)
    log_teacher = log_normalize(teacher_logits.astype(jnp.float32))
    prob_teacher = jnp.exp(log_teacher)
    prob_student = jnp.exp(log_student)
    token_total = jnp.sum(lengths).astype(jnp.float32)
    divergence = jnp.sum(token_valid * prob_teacher * (log_teacher - log_student))
    loss_value = divergence / token_total
    logit_grad = (token_valid * (prob_student - prob_teacher)).astype(jnp.bfloat16)
    reduced = lax.dot_general(logit_grad, head_weight, (((1,), (1,)), ((), ())), preferred_element_type=jnp.float32)
    grad_hidden = (reduced * (loss_scale / token_total)).astype(jnp.bfloat16)
    return grad_hidden, loss_value
```

```python
import jax
import jax.numpy as jnp
from jax import lax
from jax.sharding import PartitionSpec as P

loss_scale = 131072.0
bf16, f32 = jnp.bfloat16, jnp.float32
pad_rows = 16


def merge(parts):
    student_top, student_sum, teacher_top, teacher_sum, cross = (parts[:, i] for i in range(5))
    top_s = jnp.max(student_top, axis=0)
    top_t = jnp.max(teacher_top, axis=0)
    shift_s = student_top - top_s
    shift_t = teacher_top - top_t
    sum_s = jnp.sum(student_sum * jnp.exp(shift_s), axis=0)
    weight = jnp.exp(shift_t)
    sum_t = jnp.sum(teacher_sum * weight, axis=0)
    cross = jnp.sum(weight * (cross + teacher_sum * (shift_t - shift_s)), axis=0)
    return [top_s, sum_s, top_t, sum_t, cross]


def solution(mesh):
    rows_n, voc_n = mesh.shape["row"], mesh.shape["voc"]
    z_n = voc_n // 2
    z_groups = [[2 * z + c for z in range(z_n)] for c in range(2)]
    swap = [(i, i ^ 1) for i in range(voc_n)]

    def on_device(hidden, head_weight, teacher_logits, lengths):
        own, width = hidden.shape
        vocab = head_weight.shape[1]
        part = width // voc_n
        total_rows = rows_n * pad_rows
        v = lax.axis_index("voc")
        z, c = v // 2, v % 2

        mine = lax.dynamic_slice(hidden, (0, (c * z_n + z) * part), (own, part))
        mine = jnp.pad(mine, ((0, pad_rows - own), (0, 0)))
        mine = jnp.broadcast_to(mine[None], (rows_n, pad_rows, part))
        mine = lax.all_to_all(mine, "row", 0, 0, tiled=True).reshape(total_rows, part)
        half = lax.all_gather(mine, "voc", axis=0, axis_index_groups=z_groups)
        other = lax.ppermute(half, "voc", swap)

        teacher = teacher_logits.reshape(2, rows_n, own, -1)
        teacher = jnp.pad(teacher, ((0, 0), (0, 0), (0, pad_rows - own), (0, 0)))
        teacher = lax.all_to_all(teacher.reshape(2, total_rows, -1), "sec", 0, 0, tiled=True)
        target = jnp.concatenate([teacher[0], teacher[1]], axis=1).astype(f32)

        head = head_weight.reshape(2, z_n, part, vocab)

        def product(x, which):
            w = lax.dynamic_index_in_dim(head, which, 0, keepdims=False)
            return lax.dot_general(x, w, (((0, 2), (0, 1)), ((), ())), preferred_element_type=f32)

        student = product(half, c) + product(other, 1 - c)

        top_s = jnp.max(student, axis=1)
        top_t = jnp.max(target, axis=1)
        low_s = student - top_s[:, None]
        low_t = target - top_t[:, None]
        exp_t = jnp.exp(low_t)
        stats = jnp.stack(
            [
                top_s,
                jnp.sum(jnp.exp(low_s), axis=1),
                top_t,
                jnp.sum(exp_t, axis=1),
                jnp.sum(exp_t * (low_t - low_s), axis=1),
            ]
        )
        stats = jnp.broadcast_to(stats[None], (voc_n,) + stats.shape)
        stats = merge(lax.all_to_all(stats, "voc", 0, 0, tiled=True))
        own_length = lengths[0].astype(f32)
        stats = jnp.stack(stats + [jnp.broadcast_to(own_length, (total_rows,))])
        stats = jnp.broadcast_to(stats[None], (rows_n,) + stats.shape)
        stats = lax.all_to_all(stats, "row", 0, 0, tiled=True)
        row_lengths = stats[:, 5, 0]
        top_s, sum_s, top_t, sum_t, cross = merge(stats)

        log_s, log_t = jnp.log(sum_s), jnp.log(sum_t)
        position = jnp.arange(pad_rows, dtype=jnp.int32).astype(f32)
        valid = (position[None, :] < row_lengths[:, None]).reshape(-1)
        row_loss = jnp.where(valid, cross / sum_t + (log_s - log_t), 0.0)
        pair = jnp.stack([jnp.sum(row_loss), jnp.sum(row_lengths)])
        pair = pair + lax.ppermute(pair, "sec", [(0, 1), (1, 0)])
        loss_value = pair[0] / pair[1]

        grad = jnp.exp(student - (top_s + log_s)[:, None]) - jnp.exp(target - (top_t + log_t)[:, None])
        grad = jnp.where(valid[:, None], grad, 0.0).astype(bf16)
        back = lax.dot_general(grad, head_weight, (((1,), (1,)), ((), ())), preferred_element_type=f32)
        back = back.reshape(total_rows, z_n, 2, part).transpose(2, 1, 0, 3)
        away = lax.dynamic_index_in_dim(back, 1 - c, 0, keepdims=False).astype(bf16)
        kept = lax.dynamic_index_in_dim(back, c, 0, keepdims=False)
        kept = (kept + lax.ppermute(away, "voc", swap).astype(f32)).astype(bf16)
        kept = lax.all_to_all(kept, "voc", 0, 0, tiled=True, axis_index_groups=z_groups)
        kept = jnp.sum(kept.astype(f32), axis=0).reshape(rows_n, pad_rows, part)
        kept = lax.all_to_all(kept, "row", 0, 0, tiled=True)
        kept = jnp.sum(kept, axis=0)[:own]
        grad_hidden = (kept * (loss_scale / pair[1])).astype(bf16)
        return grad_hidden, loss_value

    in_specs = (
        P(("sec", "row"), None),
        P(None, ("row", "voc")),
        P(None, ("row", "voc", "sec")),
        P(("sec", "row")),
    )
    out_specs = (P(("sec", "row"), "voc"), P())
    return jax.shard_map(on_device, mesh=mesh, in_specs=in_specs, out_specs=out_specs, check_vma=False)
```

```python
import jax
import jax.numpy as jnp
from jax import lax
from jax.experimental import pallas as pl
from jax.experimental.pallas import tpu as pltpu
from jax.sharding import PartitionSpec as P

loss_scale = 131072.0
bf16, f32 = jnp.bfloat16, jnp.float32
pad_rows = 16


def merge(log_s, log_t, cross):
    top_s = jnp.max(log_s, axis=0, keepdims=True)
    top_t = jnp.max(log_t, axis=0, keepdims=True)
    all_s = top_s + jnp.log(jnp.sum(jnp.exp(log_s - top_s), axis=0, keepdims=True))
    all_t = top_t + jnp.log(jnp.sum(jnp.exp(log_t - top_t), axis=0, keepdims=True))
    gap = log_t - all_t
    cross = jnp.sum(jnp.exp(gap) * (cross + gap - (log_s - all_s)), axis=0, keepdims=True)
    return all_s, all_t, cross


def grad_kernel(core, stats, student, target, w_away, w_kept, away, kept, pair, grad):
    del core

    @pl.when(pl.program_id(0) == 0)
    def _():
        peers, _, rows = stats.shape
        log_s, log_t, cross = merge(stats[:, 0, :], stats[:, 1, :], stats[:, 2, :])
        lengths = stats[:, 3, :]
        owner = lax.broadcasted_iota(jnp.int32, (peers, rows), 0)
        row = lax.broadcasted_iota(jnp.int32, (peers, rows), 1)
        inside = (row // pad_rows == owner) & ((row % pad_rows).astype(f32) < lengths)
        valid = jnp.sum(jnp.where(inside, 1.0, 0.0), axis=0, keepdims=True)
        loss = jnp.sum(jnp.where(valid > 0.0, cross, 0.0), axis=1, keepdims=True)
        tokens = jnp.sum(lengths[:, :1], axis=0, keepdims=True)
        which = lax.broadcasted_iota(jnp.int32, pair.shape, 0)
        pair[...] = jnp.where(which == 0, loss, tokens)

        def column(x):
            return jnp.broadcast_to(x, (128, rows)).T[:, :1]

        prob_s = jnp.exp(student[...] - column(log_s))
        prob_t = jnp.exp(target[...].astype(f32) - column(log_t))
        grad[...] = jnp.where(column(valid) > 0.0, prob_s - prob_t, 0.0).astype(bf16)

    def product(w):
        return lax.dot_general(grad[...], w[0, 0], (((1,), (1,)), ((), ())), preferred_element_type=f32)

    away[0] = product(w_away).astype(bf16)
    kept[0] = product(w_kept)


def grad_products(core, stats, student, target, head_weight, z_n, part):
    rows, vocab = student.shape
    head = head_weight.reshape(z_n, 2, part, vocab)
    whole = lambda shape: pl.BlockSpec(shape, lambda z, core: (0,) * len(shape))
    piece = pl.BlockSpec((1, rows, part), lambda z, core: (z, 0, 0))
    return pl.pallas_call(
        grad_kernel,
        grid_spec=pltpu.PrefetchScalarGridSpec(
            num_scalar_prefetch=1,
            grid=(z_n,),
            in_specs=[
                whole(stats.shape),
                whole(student.shape),
                whole(target.shape),
                pl.BlockSpec((1, 1, part, vocab), lambda z, core: (z, 1 - core[0], 0, 0)),
                pl.BlockSpec((1, 1, part, vocab), lambda z, core: (z, core[0], 0, 0)),
            ],
            out_specs=[piece, piece, whole((8, 128))],
            scratch_shapes=[pltpu.VMEM((rows, vocab), bf16)],
        ),
        out_shape=[
            jax.ShapeDtypeStruct((z_n, rows, part), bf16),
            jax.ShapeDtypeStruct((z_n, rows, part), f32),
            jax.ShapeDtypeStruct((8, 128), f32),
        ],
        compiler_params=pltpu.CompilerParams(vmem_limit_bytes=16 * 1024 * 1024),
        cost_estimate=pl.CostEstimate(flops=2 * rows * vocab * 2 * z_n * part, bytes_accessed=8 * 2**20, transcendentals=2 * rows * vocab),
        name="grad_products",
    )(core, stats, student, target, head, head)


def solution(mesh):
    rows_n, voc_n = mesh.shape["row"], mesh.shape["voc"]
    z_n = voc_n // 2
    z_groups = [[2 * z + c for z in range(z_n)] for c in range(2)]
    swap = [(i, i ^ 1) for i in range(voc_n)]
    other_sec = [(0, 1), (1, 0)]

    def on_device(hidden, head_weight, teacher_logits, lengths):
        own, width = hidden.shape
        part = width // voc_n
        total_rows = rows_n * pad_rows
        s = lax.axis_index("sec")
        c = lax.axis_index("voc") % 2

        teacher = teacher_logits.reshape(2, rows_n, own, -1)
        teacher = jnp.pad(teacher, ((0, 0), (0, 0), (0, pad_rows - own), (0, 0)))
        teacher = teacher.reshape(2, total_rows, -1)
        t_mine = lax.dynamic_index_in_dim(teacher, s, 0, keepdims=False)
        t_away = lax.dynamic_index_in_dim(teacher, 1 - s, 0, keepdims=False)
        t_other = lax.ppermute(t_away, "sec", other_sec)
        target = jnp.where(
            s == 0, jnp.concatenate([t_mine, t_other], axis=1), jnp.concatenate([t_other, t_mine], axis=1)
        )

        mine = lax.dynamic_slice(hidden, (0, c * (width // 2)), (own, width // 2))
        mine = jnp.pad(mine, ((0, pad_rows - own), (0, 0)))
        mine = jnp.broadcast_to(mine[None], (rows_n, pad_rows, width // 2))
        half = lax.all_to_all(mine, "row", 0, 0, tiled=True).reshape(total_rows, width // 2)
        other = lax.ppermute(half, "voc", swap)

        def product(x, which):
            w = lax.dynamic_slice(head_weight, (which * (width // 2), 0), (width // 2, head_weight.shape[1]))
            return jnp.dot(x, w, preferred_element_type=f32)

        student = product(half, c) + product(other, 1 - c)

        top_s = jnp.max(student, axis=1)
        low_s = student - top_s[:, None]
        log_s = jnp.log(jnp.sum(jnp.exp(low_s), axis=1))
        wide = target.astype(f32)
        top_t = jnp.max(wide, axis=1)
        low_t = wide - top_t[:, None]
        exp_t = jnp.exp(low_t)
        sum_t = jnp.sum(exp_t, axis=1)
        log_t = jnp.log(sum_t)
        cross = jnp.sum(exp_t * (low_t - low_s), axis=1) / sum_t + (log_s - log_t)
        stats = jnp.stack([top_s + log_s, top_t + log_t, cross, cross])
        stats = jnp.broadcast_to(stats[None], (voc_n,) + stats.shape)
        stats = lax.all_to_all(stats, "voc", 0, 0, tiled=True)
        own_length = jnp.broadcast_to(lengths[0].astype(f32), (1, total_rows))
        stats = jnp.concatenate(merge(stats[:, 0], stats[:, 1], stats[:, 2]) + (own_length,), axis=0)
        stats = jnp.broadcast_to(stats[None], (rows_n,) + stats.shape)
        stats = lax.all_to_all(stats, "row", 0, 0, tiled=True)

        away, kept, pair = grad_products(
            jnp.reshape(c, (1,)).astype(jnp.int32), stats, student, target, head_weight, z_n, part
        )
        pair = pair + lax.ppermute(pair, "sec", other_sec)
        kept = (kept + lax.ppermute(away, "voc", swap).astype(f32)).astype(bf16)
        kept, pair = lax.optimization_barrier((kept, pair))
        kept = lax.all_to_all(kept, "voc", 0, 0, tiled=True, axis_index_groups=z_groups)
        kept = jnp.sum(kept.astype(f32), axis=0).reshape(rows_n, pad_rows, part)
        kept = lax.all_to_all(kept, "row", 0, 0, tiled=True)
        kept = jnp.sum(kept, axis=0)[:own]
        tokens = pair[1, 0]
        return (kept * (loss_scale / tokens)).astype(bf16), pair[0, 0] / tokens

    in_specs = (
        P(("sec", "row"), None),
        P(None, ("row", "voc")),
        P(None, ("row", "voc", "sec")),
        P(("sec", "row")),
    )
    out_specs = (P(("sec", "row"), "voc"), P())
    return jax.shard_map(on_device, mesh=mesh, in_specs=in_specs, out_specs=out_specs, check_vma=False)
```

```python
import jax
import jax.numpy as jnp
from jax import lax
from jax.experimental import pallas as pl
from jax.experimental.pallas import tpu as pltpu
from jax.sharding import PartitionSpec as P

loss_scale = 131072.0
bf16, f32 = jnp.bfloat16, jnp.float32
pad_rows = 16


def merge(log_s, log_t, cross):
    top_s = jnp.max(log_s, axis=0, keepdims=True)
    top_t = jnp.max(log_t, axis=0, keepdims=True)
    all_s = top_s + jnp.log(jnp.sum(jnp.exp(log_s - top_s), axis=0, keepdims=True))
    all_t = top_t + jnp.log(jnp.sum(jnp.exp(log_t - top_t), axis=0, keepdims=True))
    gap = log_t - all_t
    cross = jnp.sum(jnp.exp(gap) * (cross + gap - (log_s - all_s)), axis=0, keepdims=True)
    return all_s, all_t, cross


def grad_kernel(core, stats, student, target, head, away, kept, pair, w_buf, sems):
    z_n = kept.shape[0]
    copies = [pltpu.make_async_copy(head.at[v], w_buf.at[v], sems.at[v]) for v in range(2 * z_n)]
    for copy in copies:
        copy.start()

    peers, _, rows = stats.shape
    log_s, log_t, cross = merge(stats[:, 0, :], stats[:, 1, :], stats[:, 2, :])
    lengths = stats[:, 3, :]
    owner = lax.broadcasted_iota(jnp.int32, (peers, rows), 0)
    row = lax.broadcasted_iota(jnp.int32, (peers, rows), 1)
    inside = (row // pad_rows == owner) & ((row % pad_rows).astype(f32) < lengths)
    valid = jnp.sum(jnp.where(inside, 1.0, 0.0), axis=0, keepdims=True)
    loss = jnp.sum(jnp.where(valid > 0.0, cross, 0.0), axis=1, keepdims=True)
    tokens = jnp.sum(lengths[:, :1], axis=0, keepdims=True)
    which = lax.broadcasted_iota(jnp.int32, pair.shape, 0)
    pair[...] = jnp.where(which == 0, loss, tokens)

    def column(x):
        return jnp.broadcast_to(x, (128, rows)).T[:, :1]

    prob_s = jnp.exp(student[...] - column(log_s))
    prob_t = jnp.exp(target[...].astype(f32) - column(log_t))
    grad = jnp.where(column(valid) > 0.0, prob_s - prob_t, 0.0).astype(bf16)

    def product(v):
        g = lax.dot_general(grad, w_buf[v], (((1,), (1,)), ((), ())), preferred_element_type=f32)
        return g.reshape(kept.shape[1:])

    c = core[0]
    for z in range(z_n):
        copies[2 * z].wait()
        copies[2 * z + 1].wait()
        give, keep = product(2 * z + 1 - c).astype(bf16), product(2 * z + c)

        @pl.when(c == 0)
        def _():
            away[:, z] = give
            kept[z] = keep

        @pl.when(c == 1)
        def _():
            away[z] = give
            kept[:, z] = keep


def grad_products(core, stats, student, target, head_weight, z_n, part):
    rows, vocab = student.shape
    head = head_weight.reshape(2 * z_n, part, vocab)
    order = (z_n, z_n, rows // z_n, part)
    vmem = pl.BlockSpec(memory_space=pltpu.VMEM)
    return pl.pallas_call(
        grad_kernel,
        in_specs=[
            pl.BlockSpec(memory_space=pltpu.SMEM),
            vmem,
            vmem,
            vmem,
            pl.BlockSpec(memory_space=pltpu.HBM),
        ],
        out_specs=[vmem, vmem, vmem],
        scratch_shapes=[pltpu.VMEM(head.shape, bf16), pltpu.SemaphoreType.DMA((2 * z_n,))],
        out_shape=[
            jax.ShapeDtypeStruct(order, bf16),
            jax.ShapeDtypeStruct(order, f32),
            jax.ShapeDtypeStruct((8, 128), f32),
        ],
        compiler_params=pltpu.CompilerParams(vmem_limit_bytes=48 * 1024 * 1024),
        cost_estimate=pl.CostEstimate(
            flops=2 * rows * vocab * 2 * z_n * part, bytes_accessed=8 * 2**20, transcendentals=2 * rows * vocab
        ),
        name="grad_products",
    )(core, stats, student, target, head)


def solution(mesh):
    rows_n, voc_n = mesh.shape["row"], mesh.shape["voc"]
    z_n = voc_n // 2
    y_n = rows_n // 2
    assert y_n == z_n
    place = lambda y, x, z, c: (2 * y + x) * voc_n + 2 * z + c
    ys, xs, zs = range(y_n), range(2), range(z_n)
    first_groups = [[place(y, x, z, 0) for z in zs] for y in ys for x in xs]
    first_groups += [[place(y, x, z, 1) for y in ys] for z in zs for x in xs]
    last_groups = [[place(y, x, z, 0) for y in ys for x in xs] for z in zs]
    last_groups += [[place(y, x, z, 1) for z in zs for x in xs] for y in ys]
    swap = [(i, i ^ 1) for i in range(voc_n)]
    other_sec = [(0, 1), (1, 0)]

    def on_device(hidden, head_weight, teacher_logits, lengths):
        own, width = hidden.shape
        part = width // voc_n
        total_rows = rows_n * pad_rows
        s = lax.axis_index("sec")
        c = lax.axis_index("voc") % 2

        teacher = teacher_logits.reshape(2, rows_n, own, -1)
        teacher = jnp.pad(teacher, ((0, 0), (0, 0), (0, pad_rows - own), (0, 0)))
        teacher = teacher.reshape(2, total_rows, -1)
        t_mine = lax.dynamic_index_in_dim(teacher, s, 0, keepdims=False)
        t_away = lax.dynamic_index_in_dim(teacher, 1 - s, 0, keepdims=False)
        t_other = lax.ppermute(t_away, "sec", other_sec)
        target = jnp.where(
            s == 0, jnp.concatenate([t_mine, t_other], axis=1), jnp.concatenate([t_other, t_mine], axis=1)
        )

        mine = lax.dynamic_slice(hidden, (0, c * (width // 2)), (own, width // 2))
        mine = jnp.pad(mine, ((0, pad_rows - own), (0, 0)))
        mine = jnp.broadcast_to(mine[None], (rows_n, pad_rows, width // 2))
        half = lax.all_to_all(mine, "row", 0, 0, tiled=True).reshape(total_rows, width // 2)
        half, target = lax.optimization_barrier((half, target))
        other = lax.ppermute(half, "voc", swap)

        def product(x, which):
            w = lax.dynamic_slice(head_weight, (which * (width // 2), 0), (width // 2, head_weight.shape[1]))
            return jnp.dot(x, w, preferred_element_type=f32)

        student = product(half, c) + product(other, 1 - c)

        top_s = jnp.max(student, axis=1)
        low_s = student - top_s[:, None]
        log_s = jnp.log(jnp.sum(jnp.exp(low_s), axis=1))
        wide = target.astype(f32)
        top_t = jnp.max(wide, axis=1)
        low_t = wide - top_t[:, None]
        exp_t = jnp.exp(low_t)
        sum_t = jnp.sum(exp_t, axis=1)
        log_t = jnp.log(sum_t)
        cross = jnp.sum(exp_t * (low_t - low_s), axis=1) / sum_t + (log_s - log_t)
        own_length = jnp.broadcast_to(lengths[0].astype(f32), (1, total_rows))
        stats = jnp.concatenate([top_s + log_s, top_t + log_t, cross, own_length[0]]).reshape(4, total_rows)
        stats = jnp.broadcast_to(stats[None], (voc_n,) + stats.shape)
        stats = lax.all_to_all(stats, "voc", 0, 0, tiled=True)
        own_length = jnp.max(stats[:, 3], axis=0, keepdims=True)
        stats = jnp.concatenate(merge(stats[:, 0], stats[:, 1], stats[:, 2]) + (own_length,), axis=0)
        stats = jnp.broadcast_to(stats[None], (rows_n,) + stats.shape)
        stats = lax.all_to_all(stats, "row", 0, 0, tiled=True)

        away, kept, pair = grad_products(
            jnp.reshape(c, (1,)).astype(jnp.int32), stats, student, target, head_weight, z_n, part
        )
        pair = pair + lax.ppermute(pair, "sec", other_sec)
        kept = (kept + lax.ppermute(away, "voc", swap).astype(f32)).astype(bf16)
        tokens = pair[1:2, :1]
        scale, loss_value = loss_scale / tokens, pair[0, 0] / tokens[0, 0]
        kept, scale, loss_value = lax.optimization_barrier((kept, scale, loss_value))
        axes = ("row", "voc")
        kept = lax.all_to_all(kept, axes, 0, 0, tiled=True, axis_index_groups=first_groups)
        kept = jnp.sum(kept.astype(f32), axis=0).reshape(rows_n, pad_rows, part)
        kept = lax.all_to_all(kept, axes, 0, 0, tiled=True, axis_index_groups=last_groups)
        kept = jnp.sum(kept, axis=0)[:own]
        return (kept * scale).astype(bf16), loss_value

    in_specs = (
        P(("sec", "row"), None),
        P(None, ("row", "voc")),
        P(None, ("row", "voc", "sec")),
        P(("sec", "row")),
    )
    out_specs = (P(("sec", "row"), "voc"), P())
    return jax.shard_map(on_device, mesh=mesh, in_specs=in_specs, out_specs=out_specs, check_vma=False)
```

```python
import functools

import jax
import jax.numpy as jnp
from jax import lax
from jax.experimental import pallas as pl
from jax.experimental.pallas import tpu as pltpu
from jax.sharding import PartitionSpec as P

loss_scale = 131072.0
bf16, f32 = jnp.bfloat16, jnp.float32
pad_rows = 16
vmem = pl.BlockSpec(memory_space=pltpu.VMEM)
hbm = pl.BlockSpec(memory_space=pltpu.HBM)
smem = pl.BlockSpec(memory_space=pltpu.SMEM)
params = pltpu.CompilerParams(vmem_limit_bytes=24 * 1024 * 1024)


def merge(log_s, log_t, cross):
    top_s = jnp.max(log_s, axis=0, keepdims=True)
    top_t = jnp.max(log_t, axis=0, keepdims=True)
    all_s = top_s + jnp.log(jnp.sum(jnp.exp(log_s - top_s), axis=0, keepdims=True))
    all_t = top_t + jnp.log(jnp.sum(jnp.exp(log_t - top_t), axis=0, keepdims=True))
    gap = log_t - all_t
    cross = jnp.sum(jnp.exp(gap) * (cross + gap - (log_s - all_s)), axis=0, keepdims=True)
    return all_s, all_t, cross


def spread_kernel(z_n, core, hidden, out):
    own, width = hidden.shape
    part = width // (2 * z_n)
    even = core[0] == 0
    fill = jnp.zeros((out.shape[1] - own, part), f32)
    for z in range(z_n):
        both = hidden[:, 2 * z * part : 2 * (z + 1) * part].astype(f32)
        piece = jnp.where(even, both[:, :part], both[:, part:])
        piece = jnp.concatenate([piece, fill], axis=0).astype(bf16)
        out[:, :, z * part : (z + 1) * part] = jnp.broadcast_to(piece[None], out.shape[:2] + (part,))


def partial_kernel(core, x, w_mine, w_low, w_high, partial, x_buf, w_buf, sems):
    step = w_low.shape[0]
    copies = [
        pltpu.make_async_copy(x, x_buf, sems.at[0]),
        pltpu.make_async_copy(w_low, w_buf.at[:step], sems.at[1]),
        pltpu.make_async_copy(w_high, w_buf.at[step:], sems.at[2]),
    ]
    for copy in copies:
        copy.start()
    c = core[0]
    vocab = partial.shape[2]
    copies[0].wait()
    partial[c] = jnp.dot(x_buf[...], w_mine[...].reshape(-1, vocab), preferred_element_type=f32)
    copies[1].wait()
    copies[2].wait()
    partial[1 - c] = jnp.dot(x_buf[...], w_buf[...].reshape(-1, vocab), preferred_element_type=f32)


def stats_kernel(length, partial, received, target, student, stats):
    rows = student.shape[1]
    student[...] = partial[...] + received[...]
    cores = range(student.shape[0])

    def over(reduce, join, values):
        out = reduce(values[0], axis=1, keepdims=True)
        for v in values[1:]:
            out = join(out, reduce(v, axis=1, keepdims=True))
        return out

    s = [student[k] for k in cores]
    t = [target[k].astype(f32) for k in cores]
    top_s = over(jnp.max, jnp.maximum, s)
    top_t = over(jnp.max, jnp.maximum, t)
    low_s = [v - top_s for v in s]
    low_t = [v - top_t for v in t]
    exp_t = [jnp.exp(v) for v in low_t]
    log_s = jnp.log(over(jnp.sum, jnp.add, [jnp.exp(v) for v in low_s]))
    sum_t = over(jnp.sum, jnp.add, exp_t)
    log_t = jnp.log(sum_t)
    cross = over(jnp.sum, jnp.add, [e * (b - a) for e, a, b in zip(exp_t, low_s, low_t)])
    cross = cross / sum_t + (log_s - log_t)

    def line(x):
        return jnp.broadcast_to(x, (rows, 128)).T[:1]

    lines = [line(top_s + log_s), line(top_t + log_t), line(cross), jnp.full((1, rows), length[0], f32)]
    stats[...] = jnp.broadcast_to(jnp.concatenate(lines, axis=0)[None], stats.shape)


def grad_kernel(core, stats, student, target, w_mine, w_low, w_high, kept, pair, grad, w_buf, out, w_sems, out_sems):
    z_n = w_mine.shape[0]
    step = w_low.shape[0]
    peers, _, rows = stats.shape
    fetches = [
        pltpu.make_async_copy(w_low, w_buf.at[:step], w_sems.at[0]),
        pltpu.make_async_copy(w_high, w_buf.at[step:], w_sems.at[1]),
    ]
    for fetch in fetches:
        fetch.start()

    log_s, log_t, cross = merge(stats[:, 0, :], stats[:, 1, :], stats[:, 2, :])
    lengths = stats[:, 3, :]
    owner = lax.broadcasted_iota(jnp.int32, (peers, rows), 0)
    row = lax.broadcasted_iota(jnp.int32, (peers, rows), 1)
    inside = (row // pad_rows == owner) & ((row % pad_rows).astype(f32) < lengths)
    valid = jnp.sum(jnp.where(inside, 1.0, 0.0), axis=0, keepdims=True)
    loss = jnp.sum(jnp.where(valid > 0.0, cross, 0.0), axis=1, keepdims=True)
    tokens = jnp.sum(lengths[:, :1], axis=0, keepdims=True)
    which = lax.broadcasted_iota(jnp.int32, pair.shape, 0)
    pair[...] = jnp.where(which == 0, loss, tokens)

    def column(x):
        return jnp.broadcast_to(x, (128, rows)).T[:, :1]

    log_s, log_t, valid = column(log_s), column(log_t), column(valid) > 0.0
    for k in range(student.shape[0]):
        prob_s = jnp.exp(student[k] - log_s)
        prob_t = jnp.exp(target[k].astype(f32) - log_t)
        grad[k] = jnp.where(valid, prob_s - prob_t, 0.0).astype(bf16)

    c = core[0]
    mine, other = grad[c], grad[1 - c]
    dims = (((1,), (1,)), ((), ()))

    def sends(k, z):
        if k == 0:
            return [
                pltpu.make_async_copy(out.at[z, pl.ds(x * z_n, z_n)], kept.at[2 * z + x], out_sems.at[z, x])
                for x in range(2)
            ]
        return [pltpu.make_async_copy(out.at[z], kept.at[:, z], out_sems.at[z, 0])]

    for z in range(z_n):
        if z % step == 0:
            fetches[z // step].wait()
        g = lax.dot_general(mine, w_mine[z], dims, preferred_element_type=f32)
        g = g + lax.dot_general(other, w_buf[z], dims, preferred_element_type=f32)
        g = g.astype(bf16).reshape(z_n, 2, pad_rows, g.shape[1])

        @pl.when(c == 0)
        def _():
            for x in range(2):
                out[z, pl.ds(x * z_n, z_n)] = g[:, x]
            for copy in sends(0, z):
                copy.start()

        @pl.when(c == 1)
        def _():
            out[z] = g.reshape(out.shape[1:])
            for copy in sends(1, z):
                copy.start()

    for k in range(2):

        @pl.when(c == k)
        def _():
            for z in range(z_n):
                for copy in sends(k, z):
                    copy.wait()


def solution(mesh):
    rows_n, voc_n = mesh.shape["row"], mesh.shape["voc"]
    y_n, z_n = rows_n // 2, voc_n // 2
    assert y_n == z_n
    place = lambda y, x, z, c: (2 * y + x) * voc_n + 2 * z + c
    ys, xs, zs = range(y_n), range(2), range(z_n)
    z_groups = [[2 * z + c for z in zs] for c in range(2)]
    first_groups = [[place(y, x, z, 0) for z in zs for x in xs] for y in ys]
    first_groups += [[place(y, x, z, 1) for y in ys for x in xs] for z in zs]
    last_groups = [[place(y, x, z, 0) for y in ys] for x in xs for z in zs]
    last_groups += [[place(y, x, z, 1) for z in zs] for y in ys for x in xs]
    other_core = [(i, i ^ 1) for i in range(voc_n)]
    other_sec = [(0, 1), (1, 0)]

    def on_device(hidden, head_weight, teacher_logits, lengths):
        own, width = hidden.shape
        vocab = head_weight.shape[1]
        part = width // voc_n
        total_rows = rows_n * pad_rows
        s = lax.axis_index("sec")
        c = lax.axis_index("voc") % 2
        core = jnp.reshape(c, (1,)).astype(jnp.int32)
        take = lambda x, i, axis: lax.dynamic_index_in_dim(x, i, axis, keepdims=False)

        half = pl.pallas_call(
            functools.partial(spread_kernel, z_n),
            in_specs=[smem, vmem],
            out_specs=vmem,
            out_shape=jax.ShapeDtypeStruct((rows_n, pad_rows, width // 2), bf16),
            compiler_params=params,
            name="spread_rows",
        )(core, hidden)
        half, head_weight, teacher_logits = lax.optimization_barrier((half, head_weight, teacher_logits))
        half = lax.all_to_all(half, "row", 0, 0, tiled=True).reshape(total_rows, width // 2)

        teacher = teacher_logits.reshape(2, rows_n, own, -1)
        teacher = jnp.pad(teacher, ((0, 0), (0, 0), (0, pad_rows - own), (0, 0)))
        teacher = teacher.reshape(2, total_rows, -1)
        t_here, t_away = take(teacher, s, 0), take(teacher, 1 - s, 0)
        t_sec = lax.ppermute(t_away, "sec", other_sec)
        t_sec, head_weight = lax.optimization_barrier((t_sec, head_weight))
        def in_order(here, away):
            return jnp.where(s == 0, jnp.concatenate([here, away], 1), jnp.concatenate([away, here], 1))

        t_mine = in_order(t_here, t_sec)
        t_other = lax.ppermute(t_mine, "voc", other_core)
        target = jnp.where(c == 0, jnp.stack([t_mine, t_other]), jnp.stack([t_other, t_mine]))
        head = head_weight.reshape(z_n, 2, part, vocab)
        step = z_n // 2

        def rows_of(which, z, count):
            return lax.dynamic_slice(head, (z, which, 0, 0), (count, 1, part, vocab)).reshape(count, part, vocab)

        w_mine = rows_of(c, 0, z_n)
        w_low, w_high = (lax.ppermute(rows_of(1 - c, z, step), "voc", other_core) for z in (0, step))
        half, target, w_mine, w_low, w_high = lax.optimization_barrier((half, target, w_mine, w_low, w_high))

        chip = (2, total_rows, vocab)
        flops = 2 * total_rows * width * vocab
        partial = pl.pallas_call(
            partial_kernel,
            in_specs=[smem, hbm, vmem, hbm, hbm],
            out_specs=vmem,
            scratch_shapes=[
                pltpu.VMEM(half.shape, bf16),
                pltpu.VMEM(w_mine.shape, bf16),
                pltpu.SemaphoreType.DMA((3,)),
            ],
            out_shape=jax.ShapeDtypeStruct(chip, f32),
            compiler_params=params,
            cost_estimate=pl.CostEstimate(flops=flops, bytes_accessed=2**22, transcendentals=0),
            name="student_partials",
        )(core, half, w_mine, w_low, w_high)
        received = lax.ppermute(partial, "voc", other_core)
        student, stats = pl.pallas_call(
            stats_kernel,
            in_specs=[smem, vmem, vmem, vmem],
            out_specs=[vmem, vmem],
            out_shape=[jax.ShapeDtypeStruct(chip, f32), jax.ShapeDtypeStruct((z_n, 4, total_rows), f32)],
            compiler_params=params,
            cost_estimate=pl.CostEstimate(flops=2**22, bytes_accessed=2**22, transcendentals=2**19),
            name="row_statistics",
        )(lengths.astype(f32), partial, received, target)
        stats = lax.all_to_all(stats, "voc", 0, 0, tiled=True, axis_index_groups=z_groups)
        own_length = jnp.max(stats[:, 3], axis=0, keepdims=True)
        stats = jnp.concatenate(merge(stats[:, 0], stats[:, 1], stats[:, 2]) + (own_length,), axis=0)
        stats = jnp.broadcast_to(stats[None], (rows_n,) + stats.shape)
        stats = lax.all_to_all(stats, "row", 0, 0, tiled=True)

        kept, pair = pl.pallas_call(
            grad_kernel,
            in_specs=[smem] + [vmem] * 4 + [hbm] * 2,
            out_specs=[hbm, vmem],
            scratch_shapes=[
                pltpu.VMEM(chip, bf16),
                pltpu.VMEM(w_mine.shape, bf16),
                pltpu.VMEM((z_n, rows_n, pad_rows, part), bf16),
                pltpu.SemaphoreType.DMA((2,)),
                pltpu.SemaphoreType.DMA((z_n, 2)),
            ],
            out_shape=[
                pltpu.HBM((rows_n, z_n, pad_rows, part), bf16),
                jax.ShapeDtypeStruct((8, 128), f32),
            ],
            compiler_params=params,
            cost_estimate=pl.CostEstimate(flops=flops, bytes_accessed=2**23, transcendentals=2**19),
            name="grad_products",
        )(core, stats, student, target, w_mine, w_low, w_high)
        pair = pair + lax.ppermute(pair, "sec", other_sec)
        tokens = pair[1:2, :1]
        scale, loss_value = loss_scale / tokens, pair[0, 0] / tokens[0, 0]
        axes = ("row", "voc")
        kept = lax.all_to_all(kept, axes, 0, 0, tiled=True, axis_index_groups=first_groups)
        kept, scale, loss_value = lax.optimization_barrier((kept, scale, loss_value))
        kept = jnp.sum(kept.astype(f32), axis=0)
        kept = lax.all_to_all(kept, axes, 0, 0, tiled=True, axis_index_groups=last_groups)
        kept = jnp.sum(kept, axis=0)[:own]
        return (kept * scale).astype(bf16), loss_value

    in_specs = (
        P(("sec", "row"), None),
        P(None, ("row", "voc")),
        P(None, ("row", "voc", "sec")),
        P(("sec", "row")),
    )
    out_specs = (P(("sec", "row"), "voc"), P())
    return jax.shard_map(on_device, mesh=mesh, in_specs=in_specs, out_specs=out_specs, check_vma=False)
```

```python
import functools

import jax
import jax.numpy as jnp
from jax import lax
from jax.experimental import pallas as pl
from jax.experimental.pallas import tpu as pltpu
from jax.sharding import PartitionSpec as P

loss_scale = 131072.0
bf16, f32 = jnp.bfloat16, jnp.float32
pad_rows = 16
vmem = pl.BlockSpec(memory_space=pltpu.VMEM)
hbm = pl.BlockSpec(memory_space=pltpu.HBM)
smem = pl.BlockSpec(memory_space=pltpu.SMEM)
params = pltpu.CompilerParams(vmem_limit_bytes=24 * 1024 * 1024)


def merge(log_s, log_t, cross):
    top_s = jnp.max(log_s, axis=0, keepdims=True)
    top_t = jnp.max(log_t, axis=0, keepdims=True)
    all_s = top_s + jnp.log(jnp.sum(jnp.exp(log_s - top_s), axis=0, keepdims=True))
    all_t = top_t + jnp.log(jnp.sum(jnp.exp(log_t - top_t), axis=0, keepdims=True))
    gap = log_t - all_t
    cross = jnp.sum(jnp.exp(gap) * (cross + gap - (log_s - all_s)), axis=0, keepdims=True)
    return all_s, all_t, cross


def spread_kernel(z_n, core, hidden, out, block, sems):
    own, width = hidden.shape
    part = width // (2 * z_n)
    even = core[0] == 0
    fill = jnp.zeros((block.shape[0] - own, part), f32)
    for z in range(z_n):
        both = hidden[:, 2 * z * part : 2 * (z + 1) * part].astype(f32)
        piece = jnp.where(even, both[:, :part], both[:, part:])
        block[:, z * part : (z + 1) * part] = jnp.concatenate([piece, fill], axis=0).astype(bf16)
    copies = [pltpu.make_async_copy(block, out.at[p], sems.at[p]) for p in range(out.shape[0])]
    for copy in copies:
        copy.start()
    for copy in copies:
        copy.wait()


def partial_kernel(core, x, w_mine, w_low, w_high, partial, x_buf, w_buf, sems):
    step = w_low.shape[0]
    copies = [
        pltpu.make_async_copy(x, x_buf, sems.at[0]),
        pltpu.make_async_copy(w_low, w_buf.at[:step], sems.at[1]),
        pltpu.make_async_copy(w_high, w_buf.at[step:], sems.at[2]),
    ]
    for copy in copies:
        copy.start()
    c = core[0]
    vocab = partial.shape[2]
    copies[0].wait()
    partial[c] = jnp.dot(x_buf[...], w_mine[...].reshape(-1, vocab), preferred_element_type=f32)
    copies[1].wait()
    copies[2].wait()
    partial[1 - c] = jnp.dot(x_buf[...], w_buf[...].reshape(-1, vocab), preferred_element_type=f32)


def stats_kernel(length, partial, received, target, student, stats):
    rows = student.shape[1]
    student[...] = partial[...] + received[...]
    cores = range(student.shape[0])

    def over(reduce, join, values):
        out = reduce(values[0], axis=1, keepdims=True)
        for v in values[1:]:
            out = join(out, reduce(v, axis=1, keepdims=True))
        return out

    s = [student[k] for k in cores]
    t = [target[k].astype(f32) for k in cores]
    top_s = over(jnp.max, jnp.maximum, s)
    top_t = over(jnp.max, jnp.maximum, t)
    low_s = [v - top_s for v in s]
    low_t = [v - top_t for v in t]
    exp_t = [jnp.exp(v) for v in low_t]
    log_s = jnp.log(over(jnp.sum, jnp.add, [jnp.exp(v) for v in low_s]))
    sum_t = over(jnp.sum, jnp.add, exp_t)
    log_t = jnp.log(sum_t)
    cross = over(jnp.sum, jnp.add, [e * (b - a) for e, a, b in zip(exp_t, low_s, low_t)])
    cross = cross / sum_t + (log_s - log_t)

    def line(x):
        return jnp.broadcast_to(x, (rows, 128)).T[:1]

    lines = [line(top_s + log_s), line(top_t + log_t), line(cross), jnp.full((1, rows), length[0], f32)]
    stats[...] = jnp.broadcast_to(jnp.concatenate(lines, axis=0)[None], stats.shape)


def grad_kernel(core, stats, student, target, w_mine, w_low, w_high, kept, pair, grad, w_buf, out, w_sems, out_sems):
    z_n = w_mine.shape[0]
    step = w_low.shape[0]
    peers, _, rows = stats.shape
    fetches = [
        pltpu.make_async_copy(w_low, w_buf.at[:step], w_sems.at[0]),
        pltpu.make_async_copy(w_high, w_buf.at[step:], w_sems.at[1]),
    ]
    for fetch in fetches:
        fetch.start()

    log_s, log_t, cross = merge(stats[:, 0, :], stats[:, 1, :], stats[:, 2, :])
    lengths = stats[:, 3, :]
    owner = lax.broadcasted_iota(jnp.int32, (peers, rows), 0)
    row = lax.broadcasted_iota(jnp.int32, (peers, rows), 1)
    inside = (row // pad_rows == owner) & ((row % pad_rows).astype(f32) < lengths)
    valid = jnp.sum(jnp.where(inside, 1.0, 0.0), axis=0, keepdims=True)
    loss = jnp.sum(jnp.where(valid > 0.0, cross, 0.0), axis=1, keepdims=True)
    tokens = jnp.sum(lengths[:, :1], axis=0, keepdims=True)
    which = lax.broadcasted_iota(jnp.int32, pair.shape, 0)
    pair[...] = jnp.where(which == 0, loss, tokens)

    def column(x):
        return jnp.broadcast_to(x, (128, rows)).T[:, :1]

    log_s, log_t, valid = column(log_s), column(log_t), column(valid) > 0.0
    for k in range(student.shape[0]):
        prob_s = jnp.exp(student[k] - log_s)
        prob_t = jnp.exp(target[k].astype(f32) - log_t)
        grad[k] = jnp.where(valid, prob_s - prob_t, 0.0).astype(bf16)

    c = core[0]
    part, vocab = w_buf.shape[1:]
    dims = (((1,), (1,)), ((), ()))
    back = lax.dot_general(grad[c], w_mine[...].reshape(-1, vocab), dims, preferred_element_type=f32)
    for fetch in fetches:
        fetch.wait()
    back = back + lax.dot_general(grad[1 - c], w_buf[...].reshape(-1, vocab), dims, preferred_element_type=f32)

    def sends(k, z):
        if k == 0:
            return [
                pltpu.make_async_copy(out.at[z, pl.ds(x * z_n, z_n)], kept.at[2 * z + x], out_sems.at[z, x])
                for x in range(2)
            ]
        return [pltpu.make_async_copy(out.at[z], kept.at[:, z], out_sems.at[z, 0])]

    for z in range(z_n):
        g = back[:, z * part : (z + 1) * part].astype(bf16).reshape(z_n, 2, pad_rows, part)

        @pl.when(c == 0)
        def _():
            for x in range(2):
                out[z, pl.ds(x * z_n, z_n)] = g[:, x]
            for copy in sends(0, z):
                copy.start()

        @pl.when(c == 1)
        def _():
            out[z] = g.reshape(out.shape[1:])
            for copy in sends(1, z):
                copy.start()

    for k in range(2):

        @pl.when(c == k)
        def _():
            for z in range(z_n):
                for copy in sends(k, z):
                    copy.wait()


def solution(mesh):
    rows_n, voc_n = mesh.shape["row"], mesh.shape["voc"]
    y_n, z_n = rows_n // 2, voc_n // 2
    assert y_n == z_n
    place = lambda y, x, z, c: (2 * y + x) * voc_n + 2 * z + c
    ys, xs, zs = range(y_n), range(2), range(z_n)
    z_groups = [[2 * z + c for z in zs] for c in range(2)]
    first_groups = [[place(y, x, z, 0) for z in zs for x in xs] for y in ys]
    first_groups += [[place(y, x, z, 1) for y in ys for x in xs] for z in zs]
    last_groups = [[place(y, x, z, 0) for y in ys] for x in xs for z in zs]
    last_groups += [[place(y, x, z, 1) for z in zs] for y in ys for x in xs]
    other_core = [(i, i ^ 1) for i in range(voc_n)]
    other_sec = [(0, 1), (1, 0)]

    def on_device(hidden, head_weight, teacher_logits, lengths):
        own, width = hidden.shape
        vocab = head_weight.shape[1]
        part = width // voc_n
        total_rows = rows_n * pad_rows
        s = lax.axis_index("sec")
        c = lax.axis_index("voc") % 2
        core = jnp.reshape(c, (1,)).astype(jnp.int32)
        take = lambda x, i, axis: lax.dynamic_index_in_dim(x, i, axis, keepdims=False)

        half = pl.pallas_call(
            functools.partial(spread_kernel, z_n),
            in_specs=[smem, vmem],
            out_specs=hbm,
            scratch_shapes=[pltpu.VMEM((pad_rows, width // 2), bf16), pltpu.SemaphoreType.DMA((rows_n,))],
            out_shape=pltpu.HBM((rows_n, pad_rows, width // 2), bf16),
            compiler_params=params,
            name="spread_rows",
        )(core, hidden)
        half, head_weight, teacher_logits = lax.optimization_barrier((half, head_weight, teacher_logits))
        half = lax.all_to_all(half, "row", 0, 0, tiled=True).reshape(total_rows, width // 2)

        teacher = teacher_logits.reshape(2, rows_n, own, -1)
        teacher = jnp.pad(teacher, ((0, 0), (0, 0), (0, pad_rows - own), (0, 0)))
        teacher = teacher.reshape(2, total_rows, -1)
        t_here, t_away = take(teacher, s, 0), take(teacher, 1 - s, 0)
        t_sec = lax.ppermute(t_away, "sec", other_sec)
        t_sec, head_weight = lax.optimization_barrier((t_sec, head_weight))
        def in_order(here, away):
            return jnp.where(s == 0, jnp.concatenate([here, away], 1), jnp.concatenate([away, here], 1))

        t_mine = in_order(t_here, t_sec)
        t_other = lax.ppermute(t_mine, "voc", other_core)
        target = jnp.where(c == 0, jnp.stack([t_mine, t_other]), jnp.stack([t_other, t_mine]))
        head = head_weight.reshape(z_n, 2, part, vocab)
        step = z_n // 2

        def rows_of(which, z, count):
            return lax.dynamic_slice(head, (z, which, 0, 0), (count, 1, part, vocab)).reshape(count, part, vocab)

        w_mine = rows_of(c, 0, z_n)
        w_low, w_high = (lax.ppermute(rows_of(1 - c, z, step), "voc", other_core) for z in (0, step))
        half, target, w_mine, w_low, w_high = lax.optimization_barrier((half, target, w_mine, w_low, w_high))

        chip = (2, total_rows, vocab)
        flops = 2 * total_rows * width * vocab
        partial = pl.pallas_call(
            partial_kernel,
            in_specs=[smem, hbm, vmem, hbm, hbm],
            out_specs=vmem,
            scratch_shapes=[
                pltpu.VMEM(half.shape, bf16),
                pltpu.VMEM(w_mine.shape, bf16),
                pltpu.SemaphoreType.DMA((3,)),
            ],
            out_shape=jax.ShapeDtypeStruct(chip, f32),
            compiler_params=params,
            cost_estimate=pl.CostEstimate(flops=flops, bytes_accessed=2**22, transcendentals=0),
            name="student_partials",
        )(core, half, w_mine, w_low, w_high)
        received = lax.ppermute(partial, "voc", other_core)
        student, stats = pl.pallas_call(
            stats_kernel,
            in_specs=[smem, vmem, vmem, vmem],
            out_specs=[vmem, vmem],
            out_shape=[jax.ShapeDtypeStruct(chip, f32), jax.ShapeDtypeStruct((z_n, 4, total_rows), f32)],
            compiler_params=params,
            cost_estimate=pl.CostEstimate(flops=2**22, bytes_accessed=2**22, transcendentals=2**19),
            name="row_statistics",
        )(lengths.astype(f32), partial, received, target)
        stats = lax.all_to_all(stats, "voc", 0, 0, tiled=True, axis_index_groups=z_groups)
        own_length = jnp.max(stats[:, 3], axis=0, keepdims=True)
        stats = jnp.concatenate(merge(stats[:, 0], stats[:, 1], stats[:, 2]) + (own_length,), axis=0)
        stats = jnp.broadcast_to(stats[None], (rows_n,) + stats.shape)
        stats = lax.all_to_all(stats, "row", 0, 0, tiled=True)

        kept, pair = pl.pallas_call(
            grad_kernel,
            in_specs=[smem] + [vmem] * 4 + [hbm] * 2,
            out_specs=[hbm, vmem],
            scratch_shapes=[
                pltpu.VMEM(chip, bf16),
                pltpu.VMEM(w_mine.shape, bf16),
                pltpu.VMEM((z_n, rows_n, pad_rows, part), bf16),
                pltpu.SemaphoreType.DMA((2,)),
                pltpu.SemaphoreType.DMA((z_n, 2)),
            ],
            out_shape=[
                pltpu.HBM((rows_n, z_n, pad_rows, part), bf16),
                jax.ShapeDtypeStruct((8, 128), f32),
            ],
            compiler_params=params,
            cost_estimate=pl.CostEstimate(flops=flops, bytes_accessed=2**23, transcendentals=2**19),
            name="grad_products",
        )(core, stats, student, target, w_mine, w_low, w_high)
        pair = pair + lax.ppermute(pair, "sec", other_sec)
        tokens = pair[1:2, :1]
        scale, loss_value = loss_scale / tokens, pair[0, 0] / tokens[0, 0]
        axes = ("row", "voc")
        kept = lax.all_to_all(kept, axes, 0, 0, tiled=True, axis_index_groups=first_groups)
        kept, scale, loss_value = lax.optimization_barrier((kept, scale, loss_value))
        kept = jnp.sum(kept.astype(f32), axis=0)
        kept = lax.all_to_all(kept, axes, 0, 0, tiled=True, axis_index_groups=last_groups)
        kept = jnp.sum(kept, axis=0)[:own]
        return (kept * scale).astype(bf16), loss_value

    in_specs = (
        P(("sec", "row"), None),
        P(None, ("row", "voc")),
        P(None, ("row", "voc", "sec")),
        P(("sec", "row")),
    )
    out_specs = (P(("sec", "row"), "voc"), P())
    return jax.shard_map(on_device, mesh=mesh, in_specs=in_specs, out_specs=out_specs, check_vma=False)
```

```python
import functools

import jax
import jax.numpy as jnp
from jax import lax
from jax.experimental import pallas as pl
from jax.experimental.pallas import tpu as pltpu
from jax.sharding import PartitionSpec as P

loss_scale = 131072.0
bf16, f32 = jnp.bfloat16, jnp.float32
pad_rows = 16
vmem = pl.BlockSpec(memory_space=pltpu.VMEM)
hbm = pl.BlockSpec(memory_space=pltpu.HBM)
smem = pl.BlockSpec(memory_space=pltpu.SMEM)
params = pltpu.CompilerParams(vmem_limit_bytes=24 * 1024 * 1024)


def merge(log_s, log_t, cross):
    top_s = jnp.max(log_s, axis=0, keepdims=True)
    top_t = jnp.max(log_t, axis=0, keepdims=True)
    all_s = top_s + jnp.log(jnp.sum(jnp.exp(log_s - top_s), axis=0, keepdims=True))
    all_t = top_t + jnp.log(jnp.sum(jnp.exp(log_t - top_t), axis=0, keepdims=True))
    gap = log_t - all_t
    cross = jnp.sum(jnp.exp(gap) * (cross + gap - (log_s - all_s)), axis=0, keepdims=True)
    return all_s, all_t, cross


def spread_kernel(z_n, core, hidden, out, block, sems):
    own, width = hidden.shape
    part = width // (2 * z_n)
    even = core[0] == 0
    fill = jnp.zeros((block.shape[0] - own, part), f32)
    for z in range(z_n):
        both = hidden[:, 2 * z * part : 2 * (z + 1) * part].astype(f32)
        piece = jnp.where(even, both[:, :part], both[:, part:])
        block[:, z * part : (z + 1) * part] = jnp.concatenate([piece, fill], axis=0).astype(bf16)
    copies = [pltpu.make_async_copy(block, out.at[p], sems.at[p]) for p in range(out.shape[0])]
    for copy in copies:
        copy.start()
    for copy in copies:
        copy.wait()


def partial_kernel(core, x, w_mine, w_low, w_high, partial, x_buf, w_buf, sems):
    step = w_low.shape[0]
    copies = [
        pltpu.make_async_copy(x, x_buf, sems.at[0]),
        pltpu.make_async_copy(w_low, w_buf.at[:step], sems.at[1]),
        pltpu.make_async_copy(w_high, w_buf.at[step:], sems.at[2]),
    ]
    for copy in copies:
        copy.start()
    c = core[0]
    vocab = partial.shape[2]
    copies[0].wait()
    partial[c] = jnp.dot(x_buf[...], w_mine[...].reshape(-1, vocab), preferred_element_type=f32)
    copies[1].wait()
    copies[2].wait()
    partial[1 - c] = jnp.dot(x_buf[...], w_buf[...].reshape(-1, vocab), preferred_element_type=f32)


def stats_kernel(length, partial, received, target, student, stats):
    rows = student.shape[1]
    student[...] = partial[...] + received[...]
    cores = range(student.shape[0])

    def over(reduce, join, values):
        out = reduce(values[0], axis=1, keepdims=True)
        for v in values[1:]:
            out = join(out, reduce(v, axis=1, keepdims=True))
        return out

    s = [student[k] for k in cores]
    t = [target[k].astype(f32) for k in cores]
    top_s = over(jnp.max, jnp.maximum, s)
    top_t = over(jnp.max, jnp.maximum, t)
    low_s = [v - top_s for v in s]
    low_t = [v - top_t for v in t]
    exp_t = [jnp.exp(v) for v in low_t]
    log_s = jnp.log(over(jnp.sum, jnp.add, [jnp.exp(v) for v in low_s]))
    sum_t = over(jnp.sum, jnp.add, exp_t)
    log_t = jnp.log(sum_t)
    cross = over(jnp.sum, jnp.add, [e * (b - a) for e, a, b in zip(exp_t, low_s, low_t)])
    cross = cross / sum_t + (log_s - log_t)

    def line(x):
        return jnp.broadcast_to(x, (rows, 128)).T[:1]

    lines = [line(top_s + log_s), line(top_t + log_t), line(cross), jnp.full((1, rows), length[0], f32)]
    stats[...] = jnp.broadcast_to(jnp.concatenate(lines, axis=0)[None], stats.shape)


def grad_kernel(
    core, section, stats, student, target, w_mine, w_low, w_high, kept, loss, scale, grad, w_buf, w_sems
):
    z_n = w_mine.shape[0]
    step = w_low.shape[0]
    owners, rows = stats.shape[0] // 2, stats.shape[2]
    fetches = [
        pltpu.make_async_copy(w_low, w_buf.at[:step], w_sems.at[0]),
        pltpu.make_async_copy(w_high, w_buf.at[step:], w_sems.at[1]),
    ]
    for fetch in fetches:
        fetch.start()

    owner = lax.broadcasted_iota(jnp.int32, (owners, rows), 0)
    row = lax.broadcasted_iota(jnp.int32, (owners, rows), 1)
    here = row // pad_rows == owner
    position = (row % pad_rows).astype(f32)
    merged = []
    for s in range(2):
        part_of = stats[s * owners : (s + 1) * owners]
        log_s, log_t, cross = merge(part_of[:, 0, :], part_of[:, 1, :], part_of[:, 2, :])
        lengths = part_of[:, 3, :]
        valid = jnp.sum(jnp.where(here & (position < lengths), 1.0, 0.0), axis=0, keepdims=True)
        total = jnp.sum(jnp.where(valid > 0.0, cross, 0.0), axis=1, keepdims=True)
        merged.append((log_s, log_t, valid, total, jnp.sum(lengths[:, :1], axis=0, keepdims=True)))
    tokens = merged[0][4] + merged[1][4]
    loss[...] = (merged[0][3] + merged[1][3]) / tokens
    scale[...] = jnp.broadcast_to(loss_scale / tokens, scale.shape)
    first = section[0] == 0

    def column(i):
        x = jnp.where(first, merged[0][i], merged[1][i])
        return jnp.broadcast_to(x, (128, rows)).T[:, :1]

    log_s, log_t, valid = column(0), column(1), column(2) > 0.0
    for k in range(student.shape[0]):
        prob_s = jnp.exp(student[k] - log_s)
        prob_t = jnp.exp(target[k].astype(f32) - log_t)
        grad[k] = jnp.where(valid, prob_s - prob_t, 0.0).astype(bf16)

    c = core[0]
    part, vocab = w_buf.shape[1:]
    dims = (((1,), (1,)), ((), ()))
    back = lax.dot_general(grad[c], w_mine[...].reshape(-1, vocab), dims, preferred_element_type=f32)
    for fetch in fetches:
        fetch.wait()
    back = back + lax.dot_general(grad[1 - c], w_buf[...].reshape(-1, vocab), dims, preferred_element_type=f32)

    for z in range(z_n):
        g = back[:, z * part : (z + 1) * part].astype(bf16).reshape(z_n, 2, pad_rows, part)

        @pl.when(c == 0)
        def _():
            for x in range(2):
                kept[2 * z + x] = g[:, x]

        @pl.when(c == 1)
        def _():
            kept[:, z] = g.reshape(2 * z_n, pad_rows, part)


def solution(mesh):
    rows_n, voc_n = mesh.shape["row"], mesh.shape["voc"]
    y_n, z_n = rows_n // 2, voc_n // 2
    assert y_n == z_n
    place = lambda y, x, z, c: (2 * y + x) * voc_n + 2 * z + c
    ys, xs, zs = range(y_n), range(2), range(z_n)
    z_groups = [[2 * z + c for z in zs] for c in range(2)]
    first_groups = [[place(y, x, z, 0) for z in zs for x in xs] for y in ys]
    first_groups += [[place(y, x, z, 1) for y in ys for x in xs] for z in zs]
    last_groups = [[place(y, x, z, 0) for y in ys] for x in xs for z in zs]
    last_groups += [[place(y, x, z, 1) for z in zs] for y in ys for x in xs]
    other_core = [(i, i ^ 1) for i in range(voc_n)]
    other_sec = [(0, 1), (1, 0)]

    def on_device(hidden, head_weight, teacher_logits, lengths):
        own, width = hidden.shape
        vocab = head_weight.shape[1]
        part = width // voc_n
        total_rows = rows_n * pad_rows
        s = lax.axis_index("sec")
        c = lax.axis_index("voc") % 2
        core = jnp.reshape(c, (1,)).astype(jnp.int32)
        take = lambda x, i, axis: lax.dynamic_index_in_dim(x, i, axis, keepdims=False)

        half = pl.pallas_call(
            functools.partial(spread_kernel, z_n),
            in_specs=[smem, vmem],
            out_specs=hbm,
            scratch_shapes=[pltpu.VMEM((pad_rows, width // 2), bf16), pltpu.SemaphoreType.DMA((rows_n,))],
            out_shape=pltpu.HBM((rows_n, pad_rows, width // 2), bf16),
            compiler_params=params,
            name="spread_rows",
        )(core, hidden)
        half, head_weight, teacher_logits = lax.optimization_barrier((half, head_weight, teacher_logits))
        half = lax.all_to_all(half, "row", 0, 0, tiled=True).reshape(total_rows, width // 2)

        teacher = teacher_logits.reshape(2, rows_n, own, -1)
        teacher = jnp.pad(teacher, ((0, 0), (0, 0), (0, pad_rows - own), (0, 0)))
        teacher = teacher.reshape(2, total_rows, -1)
        t_here, t_away = take(teacher, s, 0), take(teacher, 1 - s, 0)
        t_sec = lax.ppermute(t_away, "sec", other_sec)
        t_sec, head_weight = lax.optimization_barrier((t_sec, head_weight))
        def in_order(here, away):
            return jnp.where(s == 0, jnp.concatenate([here, away], 1), jnp.concatenate([away, here], 1))

        t_mine = in_order(t_here, t_sec)
        t_other = lax.ppermute(t_mine, "voc", other_core)
        target = jnp.where(c == 0, jnp.stack([t_mine, t_other]), jnp.stack([t_other, t_mine]))
        head = head_weight.reshape(z_n, 2, part, vocab)
        step = z_n // 2

        def rows_of(which, z, count):
            return lax.dynamic_slice(head, (z, which, 0, 0), (count, 1, part, vocab)).reshape(count, part, vocab)

        w_mine = rows_of(c, 0, z_n)
        w_low, w_high = (lax.ppermute(rows_of(1 - c, z, step), "voc", other_core) for z in (0, step))
        half, target, w_mine, w_low, w_high = lax.optimization_barrier((half, target, w_mine, w_low, w_high))

        chip = (2, total_rows, vocab)
        flops = 2 * total_rows * width * vocab
        partial = pl.pallas_call(
            partial_kernel,
            in_specs=[smem, hbm, vmem, hbm, hbm],
            out_specs=vmem,
            scratch_shapes=[
                pltpu.VMEM(half.shape, bf16),
                pltpu.VMEM(w_mine.shape, bf16),
                pltpu.SemaphoreType.DMA((3,)),
            ],
            out_shape=jax.ShapeDtypeStruct(chip, f32),
            compiler_params=params,
            cost_estimate=pl.CostEstimate(flops=flops, bytes_accessed=2**22, transcendentals=0),
            name="student_partials",
        )(core, half, w_mine, w_low, w_high)
        received = lax.ppermute(partial, "voc", other_core)
        student, stats = pl.pallas_call(
            stats_kernel,
            in_specs=[smem, vmem, vmem, vmem],
            out_specs=[vmem, vmem],
            out_shape=[jax.ShapeDtypeStruct(chip, f32), jax.ShapeDtypeStruct((z_n, 4, total_rows), f32)],
            compiler_params=params,
            cost_estimate=pl.CostEstimate(flops=2**22, bytes_accessed=2**22, transcendentals=2**19),
            name="row_statistics",
        )(lengths.astype(f32), partial, received, target)
        stats = lax.all_to_all(stats, "voc", 0, 0, tiled=True, axis_index_groups=z_groups)
        own_length = jnp.max(stats[:, 3], axis=0, keepdims=True)
        stats = jnp.concatenate(merge(stats[:, 0], stats[:, 1], stats[:, 2]) + (own_length,), axis=0)
        stats = jnp.broadcast_to(stats[None], (2 * rows_n,) + stats.shape)
        stats = lax.all_to_all(stats, ("sec", "row"), 0, 0, tiled=True)

        kept, loss_value, scale = pl.pallas_call(
            grad_kernel,
            in_specs=[smem] * 2 + [vmem] * 4 + [hbm] * 2,
            out_specs=[vmem, vmem, vmem],
            scratch_shapes=[
                pltpu.VMEM(chip, bf16),
                pltpu.VMEM(w_mine.shape, bf16),
                pltpu.SemaphoreType.DMA((2,)),
            ],
            out_shape=[
                jax.ShapeDtypeStruct((rows_n, z_n, pad_rows, part), bf16),
                jax.ShapeDtypeStruct((1, 1), f32),
                jax.ShapeDtypeStruct((pad_rows, part), f32),
            ],
            compiler_params=params,
            cost_estimate=pl.CostEstimate(flops=flops, bytes_accessed=2**23, transcendentals=2**19),
            name="grad_products",
        )(core, jnp.reshape(s, (1,)).astype(jnp.int32), stats, student, target, w_mine, w_low, w_high)
        axes = ("row", "voc")
        kept = lax.all_to_all(kept, axes, 0, 0, tiled=True, axis_index_groups=first_groups)
        kept = jnp.sum(kept.astype(f32), axis=0)
        kept = lax.all_to_all(kept, axes, 0, 0, tiled=True, axis_index_groups=last_groups)
        kept = jnp.sum(kept, axis=0) * scale
        return kept[:own].astype(bf16), loss_value.reshape(())

    in_specs = (
        P(("sec", "row"), None),
        P(None, ("row", "voc")),
        P(None, ("row", "voc", "sec")),
        P(("sec", "row")),
    )
    out_specs = (P(("sec", "row"), "voc"), P())
    return jax.shard_map(on_device, mesh=mesh, in_specs=in_specs, out_specs=out_specs, check_vma=False)
```

```python
import functools

import jax
import jax.numpy as jnp
from jax import lax
from jax.experimental import pallas as pl
from jax.experimental.pallas import tpu as pltpu
from jax.sharding import PartitionSpec as P

loss_scale = 131072.0
bf16, f32 = jnp.bfloat16, jnp.float32
pad_rows = 16
vmem = pl.BlockSpec(memory_space=pltpu.VMEM)
hbm = pl.BlockSpec(memory_space=pltpu.HBM)
smem = pl.BlockSpec(memory_space=pltpu.SMEM)
params = pltpu.CompilerParams(vmem_limit_bytes=24 * 1024 * 1024)


def merge(log_s, log_t, cross):
    top_s = jnp.max(log_s, axis=0, keepdims=True)
    top_t = jnp.max(log_t, axis=0, keepdims=True)
    all_s = top_s + jnp.log(jnp.sum(jnp.exp(log_s - top_s), axis=0, keepdims=True))
    all_t = top_t + jnp.log(jnp.sum(jnp.exp(log_t - top_t), axis=0, keepdims=True))
    gap = log_t - all_t
    cross = jnp.sum(jnp.exp(gap) * (cross + gap - (log_s - all_s)), axis=0, keepdims=True)
    return all_s, all_t, cross


def spread_kernel(z_n, core, hidden, out, block, sems):
    own, width = hidden.shape
    part = width // (2 * z_n)
    even = core[0] == 0
    fill = jnp.zeros((block.shape[0] - own, part), f32)
    for z in range(z_n):
        both = hidden[:, 2 * z * part : 2 * (z + 1) * part].astype(f32)
        piece = jnp.where(even, both[:, :part], both[:, part:])
        block[:, z * part : (z + 1) * part] = jnp.concatenate([piece, fill], axis=0).astype(bf16)
    copies = [pltpu.make_async_copy(block, out.at[p], sems.at[p]) for p in range(out.shape[0])]
    for copy in copies:
        copy.start()
    for copy in copies:
        copy.wait()


def partial_kernel(core, x, w_mine, w_low, w_high, partial, x_buf, w_buf, sems):
    step = w_low.shape[0]
    wide = x.shape[1] // 2
    copies = [
        pltpu.make_async_copy(x.at[:, :wide], x_buf.at[:, :wide], sems.at[0]),
        pltpu.make_async_copy(x.at[:, wide:], x_buf.at[:, wide:], sems.at[1]),
        pltpu.make_async_copy(w_low, w_buf.at[:step], sems.at[2]),
        pltpu.make_async_copy(w_high, w_buf.at[step:], sems.at[3]),
    ]
    for copy in copies:
        copy.start()
    c = core[0]
    vocab = partial.shape[2]
    copies[0].wait()
    first = jnp.dot(x_buf[:, :wide], w_mine[:step].reshape(-1, vocab), preferred_element_type=f32)
    copies[1].wait()
    partial[c] = first + jnp.dot(x_buf[:, wide:], w_mine[step:].reshape(-1, vocab), preferred_element_type=f32)
    copies[2].wait()
    copies[3].wait()
    partial[1 - c] = jnp.dot(x_buf[...], w_buf[...].reshape(-1, vocab), preferred_element_type=f32)


def stats_kernel(length, partial, received, target, student, stats):
    rows = student.shape[1]
    student[...] = partial[...] + received[...]
    cores = range(student.shape[0])

    def over(reduce, join, values):
        out = reduce(values[0], axis=1, keepdims=True)
        for v in values[1:]:
            out = join(out, reduce(v, axis=1, keepdims=True))
        return out

    s = [student[k] for k in cores]
    t = [target[k].astype(f32) for k in cores]
    top_s = over(jnp.max, jnp.maximum, s)
    top_t = over(jnp.max, jnp.maximum, t)
    low_s = [v - top_s for v in s]
    low_t = [v - top_t for v in t]
    exp_t = [jnp.exp(v) for v in low_t]
    log_s = jnp.log(over(jnp.sum, jnp.add, [jnp.exp(v) for v in low_s]))
    sum_t = over(jnp.sum, jnp.add, exp_t)
    log_t = jnp.log(sum_t)
    cross = over(jnp.sum, jnp.add, [e * (b - a) for e, a, b in zip(exp_t, low_s, low_t)])
    cross = cross / sum_t + (log_s - log_t)

    def line(x):
        return jnp.broadcast_to(x, (rows, 128)).T[:1]

    lines = [line(top_s + log_s), line(top_t + log_t), line(cross), jnp.full((1, rows), length[0], f32)]
    stats[...] = jnp.broadcast_to(jnp.concatenate(lines, axis=0)[None], stats.shape)


def grad_kernel(
    core, section, stats, student, target, w_mine, w_low, w_high, kept, loss, scale, grad, w_buf, w_sems
):
    z_n = w_mine.shape[0]
    step = w_low.shape[0]
    owners, rows = stats.shape[0] // 2, stats.shape[2]
    fetches = [
        pltpu.make_async_copy(w_low, w_buf.at[:step], w_sems.at[0]),
        pltpu.make_async_copy(w_high, w_buf.at[step:], w_sems.at[1]),
    ]
    for fetch in fetches:
        fetch.start()

    owner = lax.broadcasted_iota(jnp.int32, (owners, rows), 0)
    row = lax.broadcasted_iota(jnp.int32, (owners, rows), 1)
    here = row // pad_rows == owner
    position = (row % pad_rows).astype(f32)
    merged = []
    for s in range(2):
        part_of = stats[s * owners : (s + 1) * owners]
        log_s, log_t, cross = merge(part_of[:, 0, :], part_of[:, 1, :], part_of[:, 2, :])
        lengths = part_of[:, 3, :]
        valid = jnp.sum(jnp.where(here & (position < lengths), 1.0, 0.0), axis=0, keepdims=True)
        total = jnp.sum(jnp.where(valid > 0.0, cross, 0.0), axis=1, keepdims=True)
        merged.append((log_s, log_t, valid, total, jnp.sum(lengths[:, :1], axis=0, keepdims=True)))
    tokens = merged[0][4] + merged[1][4]
    loss[...] = (merged[0][3] + merged[1][3]) / tokens
    scale[...] = jnp.broadcast_to(loss_scale / tokens, scale.shape)
    first = section[0] == 0

    def column(i):
        x = jnp.where(first, merged[0][i], merged[1][i])
        return jnp.broadcast_to(x, (128, rows)).T[:, :1]

    log_s, log_t, valid = column(0), column(1), column(2) > 0.0
    for k in range(student.shape[0]):
        prob_s = jnp.exp(student[k] - log_s)
        prob_t = jnp.exp(target[k].astype(f32) - log_t)
        grad[k] = jnp.where(valid, prob_s - prob_t, 0.0).astype(bf16)

    c = core[0]
    part, vocab = w_buf.shape[1:]
    dims = (((1,), (1,)), ((), ()))
    back = lax.dot_general(grad[c], w_mine[...].reshape(-1, vocab), dims, preferred_element_type=f32)
    for fetch in fetches:
        fetch.wait()
    back = back + lax.dot_general(grad[1 - c], w_buf[...].reshape(-1, vocab), dims, preferred_element_type=f32)

    for z in range(z_n):
        g = back[:, z * part : (z + 1) * part].astype(bf16).reshape(z_n, 2, pad_rows, part)

        @pl.when(c == 0)
        def _():
            for x in range(2):
                kept[2 * z + x] = g[:, x]

        @pl.when(c == 1)
        def _():
            kept[:, z] = g.reshape(2 * z_n, pad_rows, part)


def solution(mesh):
    rows_n, voc_n = mesh.shape["row"], mesh.shape["voc"]
    y_n, z_n = rows_n // 2, voc_n // 2
    assert y_n == z_n
    place = lambda y, x, z, c: (2 * y + x) * voc_n + 2 * z + c
    ys, xs, zs = range(y_n), range(2), range(z_n)
    z_groups = [[2 * z + c for z in zs] for c in range(2)]
    first_groups = [[place(y, x, z, 0) for z in zs for x in xs] for y in ys]
    first_groups += [[place(y, x, z, 1) for y in ys for x in xs] for z in zs]
    last_groups = [[place(y, x, z, 0) for y in ys] for x in xs for z in zs]
    last_groups += [[place(y, x, z, 1) for z in zs] for y in ys for x in xs]
    other_core = [(i, i ^ 1) for i in range(voc_n)]
    other_sec = [(0, 1), (1, 0)]

    def on_device(hidden, head_weight, teacher_logits, lengths):
        own, width = hidden.shape
        vocab = head_weight.shape[1]
        part = width // voc_n
        total_rows = rows_n * pad_rows
        s = lax.axis_index("sec")
        c = lax.axis_index("voc") % 2
        core = jnp.reshape(c, (1,)).astype(jnp.int32)
        take = lambda x, i, axis: lax.dynamic_index_in_dim(x, i, axis, keepdims=False)

        half = pl.pallas_call(
            functools.partial(spread_kernel, z_n),
            in_specs=[smem, vmem],
            out_specs=hbm,
            scratch_shapes=[pltpu.VMEM((pad_rows, width // 2), bf16), pltpu.SemaphoreType.DMA((rows_n,))],
            out_shape=pltpu.HBM((rows_n, pad_rows, width // 2), bf16),
            compiler_params=params,
            name="spread_rows",
        )(core, pltpu.with_memory_space_constraint(hidden, pltpu.HBM))
        half, head_weight, teacher_logits = lax.optimization_barrier((half, head_weight, teacher_logits))
        half = lax.all_to_all(half, "row", 0, 0, tiled=True).reshape(total_rows, width // 2)

        teacher = teacher_logits.reshape(2, rows_n, own, -1)
        teacher = jnp.pad(teacher, ((0, 0), (0, 0), (0, pad_rows - own), (0, 0)))
        teacher = teacher.reshape(2, total_rows, -1)
        t_here, t_away = take(teacher, s, 0), take(teacher, 1 - s, 0)
        t_sec = lax.ppermute(t_away, "sec", other_sec)
        t_sec, head_weight = lax.optimization_barrier((t_sec, head_weight))
        def in_order(here, away):
            return jnp.where(s == 0, jnp.concatenate([here, away], 1), jnp.concatenate([away, here], 1))

        t_mine = in_order(t_here, t_sec)
        t_other = lax.ppermute(t_mine, "voc", other_core)
        target = jnp.where(c == 0, jnp.stack([t_mine, t_other]), jnp.stack([t_other, t_mine]))
        head = head_weight.reshape(z_n, 2, part, vocab)
        step = z_n // 2

        def rows_of(which, z, count):
            return lax.dynamic_slice(head, (z, which, 0, 0), (count, 1, part, vocab)).reshape(count, part, vocab)

        w_mine = rows_of(c, 0, z_n)
        w_low, w_high = (lax.ppermute(rows_of(1 - c, z, step), "voc", other_core) for z in (0, step))
        half, target, w_mine, w_low, w_high = lax.optimization_barrier((half, target, w_mine, w_low, w_high))

        chip = (2, total_rows, vocab)
        flops = 2 * total_rows * width * vocab
        partial = pl.pallas_call(
            partial_kernel,
            in_specs=[smem, hbm, vmem, hbm, hbm],
            out_specs=vmem,
            scratch_shapes=[
                pltpu.VMEM(half.shape, bf16),
                pltpu.VMEM(w_mine.shape, bf16),
                pltpu.SemaphoreType.DMA((4,)),
            ],
            out_shape=jax.ShapeDtypeStruct(chip, f32),
            compiler_params=params,
            cost_estimate=pl.CostEstimate(flops=flops, bytes_accessed=2**22, transcendentals=0),
            name="student_partials",
        )(core, half, w_mine, w_low, w_high)
        received = lax.ppermute(partial, "voc", other_core)
        student, stats = pl.pallas_call(
            stats_kernel,
            in_specs=[smem, vmem, vmem, vmem],
            out_specs=[vmem, vmem],
            out_shape=[jax.ShapeDtypeStruct(chip, f32), jax.ShapeDtypeStruct((z_n, 4, total_rows), f32)],
            compiler_params=params,
            cost_estimate=pl.CostEstimate(flops=2**22, bytes_accessed=2**22, transcendentals=2**19),
            name="row_statistics",
        )(lengths.astype(f32), partial, received, target)
        stats = lax.all_to_all(stats, "voc", 0, 0, tiled=True, axis_index_groups=z_groups)
        own_length = jnp.max(stats[:, 3], axis=0, keepdims=True)
        stats = jnp.concatenate(merge(stats[:, 0], stats[:, 1], stats[:, 2]) + (own_length,), axis=0)
        stats = jnp.broadcast_to(stats[None], (2 * rows_n,) + stats.shape)
        stats = lax.all_to_all(stats, ("sec", "row"), 0, 0, tiled=True)

        kept, loss_value, scale = pl.pallas_call(
            grad_kernel,
            in_specs=[smem] * 2 + [vmem] * 4 + [hbm] * 2,
            out_specs=[vmem, vmem, vmem],
            scratch_shapes=[
                pltpu.VMEM(chip, bf16),
                pltpu.VMEM(w_mine.shape, bf16),
                pltpu.SemaphoreType.DMA((2,)),
            ],
            out_shape=[
                jax.ShapeDtypeStruct((rows_n, z_n, pad_rows, part), bf16),
                jax.ShapeDtypeStruct((1, 1), f32),
                jax.ShapeDtypeStruct((pad_rows, part), f32),
            ],
            compiler_params=params,
            cost_estimate=pl.CostEstimate(flops=flops, bytes_accessed=2**23, transcendentals=2**19),
            name="grad_products",
        )(core, jnp.reshape(s, (1,)).astype(jnp.int32), stats, student, target, w_mine, w_low, w_high)
        axes = ("row", "voc")
        kept = lax.all_to_all(kept, axes, 0, 0, tiled=True, axis_index_groups=first_groups)
        kept = jnp.sum(kept.astype(f32), axis=0)
        kept = lax.all_to_all(kept, axes, 0, 0, tiled=True, axis_index_groups=last_groups)
        kept = jnp.sum(kept, axis=0) * scale
        return kept[:own].astype(bf16), loss_value.reshape(())

    in_specs = (
        P(("sec", "row"), None),
        P(None, ("row", "voc")),
        P(None, ("row", "voc", "sec")),
        P(("sec", "row")),
    )
    out_specs = (P(("sec", "row"), "voc"), P())
    return jax.shard_map(on_device, mesh=mesh, in_specs=in_specs, out_specs=out_specs, check_vma=False)
```
